512 devices in a mesh: section: 2 (over core), ha: 8 (over z_hi, x), wa: 32 (over z_lo, y).
Axes of the slice: x: 4, y: 8, z: 8 (z_hi: 2, z_lo: 4; z = z_hi * 4 + z_lo), core: 2. Of those that a mesh axis runs over, the one named last changes fastest.
Arguments:
- slide_tiles: bfloat16 [2, 96, 128, 4096], P('section', None, 'ha', 'wa'), may hold values from -6 to 6
- depth_kernel: float32 [3, 96, 7, 7], replicated, may hold values from -0.875 to 0.875
- depth_bias: float32 [3, 96], replicated, may hold values from -3 to 3
- norm_gain: float32 [3, 96], replicated, may hold values from 0.5 to 2
- norm_shift: float32 [3, 96], replicated, may hold values from -3 to 3
- expand_weight: bfloat16 [3, 96, 384], P(None, None, 'section'), may hold values from -0.625 to 0.625
- expand_bias: float32 [3, 384], replicated, may hold values from -3 to 3
- project_weight: bfloat16 [3, 384, 96], P(None, 'section'), may hold values from -0.3125 to 0.3125
- project_bias: float32 [3, 96], replicated, may hold values from -3 to 3
- layer_scale: float32 [3, 96], replicated, may hold values from 0.3 to 1.5
Outputs:
- section_output: bfloat16 [2, 96, 128, 4096], P('section', None, 'ha', 'wa')
The draws below stay inside these ranges and needn't reach their ends.
All inputs are finite; a program needn't handle non-finite values.
Results may differ from the reference program's by a relative error of at most 0.014.
Values may be sent and summed in bfloat16 or wider, within the bound.
A program may use at most 64 MiB of HBM per device.

```python
import math
import jax
import jax.numpy as jnp
from jax import lax

DIM = 96
MLP = 384
TILE_H = 16
BLOCKS = 3
MICRO = 2
HEIGHT = 128
WIDTH = 4096


def level_of(own_key, dims, cuts, least, largest):
    factor_of, own = 1.0, jax.random.fold_in(own_key, 6)
    for dim, blocks in cuts:
        steps = jnp.exp(jax.random.uniform(jax.random.fold_in(own, dim), (blocks,), jnp.float32, least / len(cuts), largest / len(cuts)))
        factor_of = factor_of * jnp.repeat(steps, dims[dim] // blocks).reshape([-1 if axis == dim else 1 for axis in range(len(dims))])
    return factor_of


def scatter_about(own_key, shape, deviation, most, split=(), kind=jnp.bfloat16):
    factor_of = level_of(own_key, shape, split, -0.22, 0.18) if split else 1.0
    entries = jax.random.normal(own_key, shape, jnp.float32) * deviation * factor_of
    return jnp.minimum(jnp.maximum(entries, -most), most).astype(kind)


def setup_inputs(seed: int = 0) -> dict:
    key_list = jax.random.split(jax.random.key(seed), 11)
    slide_tiles = scatter_about(key_list[0], (MICRO, DIM, HEIGHT, WIDTH), 1.0, 6.0, ((0, 2), (2, 8), (3, 32)))
    depth_kernel = scatter_about(key_list[1], (BLOCKS, DIM, 7, 7), 49 ** -0.5, 0.875, (), jnp.float32)
    depth_bias = scatter_about(key_list[2], (BLOCKS, DIM), 0.5, 3.0, (), jnp.float32)
    norm_gain = jnp.clip(jnp.exp(jax.random.uniform(key_list[3], (BLOCKS, DIM), jnp.float32, math.log(0.5), math.log(2.0))), 0.5, 2.0)
    norm_shift = scatter_about(key_list[4], (BLOCKS, DIM), 0.5, 3.0, (), jnp.float32)
    expand_weight = scatter_about(key_list[5], (BLOCKS, DIM, MLP), DIM ** -0.5, 0.625, ((2, 2),))
    expand_bias = scatter_about(key_list[6], (BLOCKS, MLP), 0.5, 3.0, (), jnp.float32)
    project_weight = scatter_about(key_list[7], (BLOCKS, MLP, DIM), MLP ** -0.5, 0.3125, ((1, 2),))
    project_bias = scatter_about(key_list[8], (BLOCKS, DIM), 0.5, 3.0, (), jnp.float32)
    layer_scale = jnp.clip(jnp.exp(jax.random.uniform(key_list[9], (BLOCKS, DIM), jnp.float32, math.log(0.3), math.log(1.5))), 0.3, 1.5)
    return dict(slide_tiles=slide_tiles, depth_kernel=depth_kernel, depth_bias=depth_bias, norm_gain=norm_gain, norm_shift=norm_shift, expand_weight=expand_weight, expand_bias=expand_bias, project_weight=project_weight, project_bias=project_bias, layer_scale=layer_scale)


epsilon = 1e-06

def convnext_block(padded, kernel, dbias, gain, shift, w_in, b_in, w_out, b_out, scale):
    channels = padded.shape[0]
    height = padded.shape[1] - 6
    width = padded.shape[2] - 6
    summed = jnp.zeros((channels, height, width), jnp.float32) + dbias[:, None, None]
    for row_off in range(7):
        for col_off in range(7):
            window = padded[:, row_off:row_off + height, col_off:col_off + width].astype(jnp.float32)
            summed = summed + window * kernel[:, row_off, col_off][:, None, None]
    average = lax.optimization_barrier(jnp.mean(summed, axis=0))
    centred = summed - average
    variance = lax.optimization_barrier(jnp.mean(centred * centred, axis=0))
    normed = (centred * lax.rsqrt(variance + epsilon) * gain[:, None, None] + shift[:, None, None]).astype(jnp.bfloat16)
    flattened = normed.reshape(channels, height * width)
    hidden_units = jnp.dot(w_in.T, flattened, preferred_element_type=jnp.float32) + b_in[:, None]
    activated = jax.nn.gelu(hidden_units, approximate=False).astype(jnp.bfloat16)
    projected = jnp.dot(w_out.T, activated, preferred_element_type=jnp.float32) + b_out[:, None]
    centre = padded[:, 3:3 + height, 3:3 + width].astype(jnp.float32)
    return (centre + scale[:, None, None] * projected.reshape(channels, height, width)).astype(jnp.bfloat16)

def apply_layer(image, params):
    padded = jnp.pad(image, ((0, 0), (3, 3), (3, 3)))
    bands = HEIGHT // TILE_H

    def one_band(index):
        start = (index * TILE_H).astype(jnp.int32)
        piece = lax.dynamic_slice_in_dim(padded, start, TILE_H + 6, 1)
        return convnext_block(piece, *params)
    stacked = lax.map(one_band, jnp.arange(bands, dtype=jnp.int32))
    return jnp.transpose(stacked, (1, 0, 2, 3)).reshape(DIM, HEIGHT, WIDTH)

def reference(slide_tiles, depth_kernel, depth_bias, norm_gain, norm_shift, expand_weight, expand_bias, project_weight, project_bias, layer_scale):
    results = []
    for micro_no in range(MICRO):
        image = slide_tiles[micro_no]
        for layer_no in range(BLOCKS):
            params = (depth_kernel[layer_no], depth_bias[layer_no], norm_gain[layer_no], norm_shift[layer_no], expand_weight[layer_no], expand_bias[layer_no], project_weight[layer_no], project_bias[layer_no], layer_scale[layer_no])
            image = apply_layer(image, params)
        results.append(image)
    return jnp.stack(results)
```

```python
import functools

import jax
import jax.numpy as jnp
from jax import lax
from jax.experimental import pallas as pl
from jax.experimental.pallas import tpu as pltpu
from jax.sharding import PartitionSpec as P

EPSILON = 1e-06
MESH = pl.DeviceIdType.MESH
BF16, F32 = jnp.bfloat16, jnp.float32

AROUND = ((-1, -1), (-1, 0), (-1, 1), (0, -1), (0, 1), (1, -1), (1, 0), (1, 1))
UP, DOWN = 1, 6
REACH = 3
ROWS = 4


def columns_of(row):
    return jnp.broadcast_to(row, (128, row.shape[1])).T


def kernel(
    axis_sizes,
    tile_ref,
    taps_ref,
    dbias_ref,
    gain_ref,
    shift_ref,
    expand_ref,
    ebias_ref,
    project_ref,
    pbias_ref,
    scale_ref,
    out_ref,
    state,
    packed,
    row_halo,
    col_halo,
    shifted,
    taps,
    vectors,
    first,
    second,
    conv,
    normed,
    send_sem,
    recv_sem,
    wsend_sem,
    wrecv_sem,
):
    blocks = packed.shape[0]
    rows, channels = state.shape[1], state.shape[2]
    half = first.shape[2]
    section, ha, wa = (lax.axis_index(a) for a in ("section", "ha", "wa"))
    n_ha, n_wa = axis_sizes
    here = []
    for dy, dx in AROUND:
        inside = jnp.bool_(True)
        if dy:
            inside = jnp.logical_and(inside, ha > 0 if dy < 0 else ha < n_ha - 1)
        if dx:
            inside = jnp.logical_and(inside, wa > 0 if dx < 0 else wa < n_wa - 1)
        here.append(inside)

    def device(d):
        dy, dx = AROUND[d]
        return (section, ha + dy, wa + dx)

    row_halo[...] = jnp.zeros_like(row_halo)
    col_halo[...] = jnp.zeros_like(col_halo)

    barrier = pltpu.get_barrier_semaphore()
    for d in range(8):

        @pl.when(here[d])
        def _(d=d):
            pl.semaphore_signal(barrier, inc=1, device_id=device(d), device_id_type=MESH)

    partner = (1 - section, ha, wa)
    pl.semaphore_signal(barrier, inc=1, device_id=partner, device_id_type=MESH)

    for b in range(blocks):
        bias = jnp.where(section == 0, ebias_ref[b : b + 1, :half], ebias_ref[b : b + 1, half:])
        parts = []
        for _ in range(3):
            part = bias.astype(BF16).astype(F32)
            bias = bias - part
            parts.append(part)
        whole = jnp.concatenate(
            [expand_ref[b].astype(F32)] + parts + [jnp.zeros((128 - channels - 3, half), F32)], axis=0
        )
        first[0, b] = whole.T.astype(BF16)
        second[0, b] = project_ref[b].astype(F32).T.astype(BF16)
        scale = scale_ref[b : b + 1, :]
        for k, row in enumerate(
            (dbias_ref[b : b + 1, :], gain_ref[b : b + 1, :], shift_ref[b : b + 1, :], scale, scale * pbias_ref[b : b + 1, :])
        ):
            vectors[b, k] = columns_of(row)

    def spread(i, carry):
        for b in range(blocks):
            for j in range(7):
                taps[b, i * 7 + j] = columns_of(taps_ref[b, i, j : j + 1, :])
        return carry

    lax.fori_loop(0, 7, spread, 0)
    ones = lax.broadcasted_iota(jnp.int32, (128 - channels, ROWS * 128), 0) < 3
    normed[channels:, :] = jnp.where(ones, 1.0, 0.0).astype(BF16)
    state[0] = jnp.swapaxes(tile_ref[...], 0, 1)

    lane = lax.broadcasted_iota(jnp.int32, (channels, 128), 1)

    def pack(b):
        kept = jnp.zeros((channels, 128), BF16)
        for h in range(rows):
            kept = jnp.where(lane // 8 == h, pltpu.roll(state[b, h], 8 * h + REACH, 1), kept)
        packed[b] = kept

    pack(0)
    greeted = jnp.int32(1)
    for d in range(8):
        greeted = greeted + here[d].astype(jnp.int32)
    pl.semaphore_wait(barrier, greeted)

    weights = [
        pltpu.make_async_remote_copy(
            src_ref=ref.at[0], dst_ref=ref.at[1], send_sem=wsend_sem.at[k], recv_sem=wrecv_sem.at[k],
            device_id=partner, device_id_type=MESH,
        )
        for k, ref in enumerate((first, second))
    ]

    def copy(b, d):
        if d == UP:
            source, target = state.at[b, pl.ds(0, REACH)], row_halo.at[b, 1]
        elif d == DOWN:
            source, target = state.at[b, pl.ds(rows - REACH, REACH)], row_halo.at[b, 0]
        else:
            source, target = packed.at[b], col_halo.at[b, 7 - d]
        return pltpu.make_async_remote_copy(
            src_ref=source, dst_ref=target, send_sem=send_sem.at[b, d], recv_sem=recv_sem.at[b, 7 - d],
            device_id=device(d), device_id_type=MESH,
        )

    def send(b):
        for d in (3, 4, UP, DOWN, 0, 2, 5, 7):

            @pl.when(here[d])
            def _(d=d):
                copy(b, d).start()

    def receive(b, which):
        for d in which:

            @pl.when(here[d])
            def _(d=d):
                copy(b, 7 - d).wait_recv()

    def lay_out(b, at, row, ends):
        for j in range(7):
            s = REACH - j
            if s > 0:
                moved = pltpu.roll(jnp.where(lane >= 128 - s, ends, row), s, 1)
            elif s < 0:
                moved = pltpu.roll(jnp.where(lane < -s, ends, row), 128 + s, 1)
            else:
                moved = row
            shifted[j, at] = moved.astype(F32)

    def ends_of(b, left, right, h):
        both = jnp.where(lane % 8 < REACH, col_halo[b, left], col_halo[b, right])
        return pltpu.roll(both, 128 - (8 * h + REACH), 1)

    def chunk(b, at):
        def group(g, carry):
            part = pl.ds(pl.multiple_of(g * 8, 8), 8)
            total = jnp.broadcast_to(vectors[b, 0, part, :][None], (ROWS, 8, 128))
            for j in range(7):
                source = shifted[j, pl.ds(at, ROWS + 6), part, :]
                for i in range(7):
                    total = total + source[i : i + ROWS] * taps[b, i * 7 + j, part, :][None]
            conv[:, part, :] = total
            return carry

        lax.fori_loop(0, channels // 8, group, 0)
        for k in range(ROWS):
            value = conv[k]
            centred = value - jnp.mean(value, axis=0, keepdims=True)
            variance = jnp.mean(centred * centred, axis=0, keepdims=True)
            normed[:channels, k * 128 : (k + 1) * 128] = (
                centred * lax.rsqrt(variance + EPSILON) * vectors[b, 1] + vectors[b, 2]
            ).astype(BF16)
        projected = None
        for s in range(2):
            hidden = jnp.dot(first[s, b], normed[...], preferred_element_type=F32)
            activated = (0.5 * hidden * (1.0 + lax.erf(hidden * (2.0**-0.5)))).astype(BF16)
            part = jnp.dot(second[s, b], activated, preferred_element_type=F32)
            projected = part if projected is None else projected + part
        for k in range(ROWS):
            value = (
                state[b, at + k].astype(F32)
                + vectors[b, 3] * projected[:, k * 128 : (k + 1) * 128]
                + vectors[b, 4]
            ).astype(BF16)
            state[b + 1, at + k] = value

    send(0)
    for copy_of in weights:
        copy_of.start()
    for b in range(blocks):
        receive(b, (3, 4))
        for h in range(rows):
            lay_out(b, REACH + h, state[b, h], ends_of(b, 3, 4, h))
        if b == 0:
            for copy_of in weights:
                copy_of.wait_recv()

        def middle(c, carry, b=b):
            chunk(b, c * ROWS)
            return carry

        lax.fori_loop(1, rows // ROWS - 1, middle, 0)
        receive(b, (0, 1, 2, 5, 6, 7))
        for k in range(REACH):
            lay_out(b, k, row_halo[b, 0, k], ends_of(b, 0, 2, rows - REACH + k))
            lay_out(b, rows + REACH + k, row_halo[b, 1, k], ends_of(b, 5, 7, k))

        def outer(c, carry, b=b):
            chunk(b, c * (rows - ROWS))
            return carry

        lax.fori_loop(0, 2, outer, 0)
        if b + 1 < blocks:
            pack(b + 1)
            send(b + 1)
    out_ref[...] = jnp.swapaxes(state[blocks], 0, 1)

    for copy_of in weights:
        copy_of.wait_send()
    for b in range(blocks):
        for d in range(8):

            @pl.when(here[d])
            def _(b=b, d=d):
                copy(b, d).wait_send()


def solution(mesh):
    n_ha, n_wa = mesh.shape["ha"], mesh.shape["wa"]

    def body(tiles, taps, dbias, gain, shift, expand, ebias, project, pbias, scale):
        blocks, channels = dbias.shape
        rows, width = tiles.shape[2:]
        half = expand.shape[2]
        vmem = pl.BlockSpec(memory_space=pltpu.VMEM)
        result = pl.pallas_call(
            functools.partial(kernel, (n_ha, n_wa)),
            out_shape=jax.ShapeDtypeStruct((channels, rows, width), BF16),
            in_specs=[vmem] * 10,
            out_specs=vmem,
            scratch_shapes=[
                pltpu.VMEM((blocks + 1, rows, channels, width), BF16),
                pltpu.VMEM((blocks, channels, width), BF16),
                pltpu.VMEM((blocks, 2, REACH, channels, width), BF16),
                pltpu.VMEM((blocks, 8, channels, width), BF16),
                pltpu.VMEM((7, rows + 2 * REACH, channels, width), F32),
                pltpu.VMEM((blocks, 49, channels, 128), F32),
                pltpu.VMEM((blocks, 5, channels, 128), F32),
                pltpu.VMEM((2, blocks, half, 128), BF16),
                pltpu.VMEM((2, blocks, channels, half), BF16),
                pltpu.VMEM((ROWS, channels, width), F32),
                pltpu.VMEM((128, ROWS * width), BF16),
                pltpu.SemaphoreType.DMA((blocks, 8)),
                pltpu.SemaphoreType.DMA((blocks, 8)),
                pltpu.SemaphoreType.DMA((2,)),
                pltpu.SemaphoreType.DMA((2,)),
            ],
            compiler_params=pltpu.CompilerParams(
                collective_id=0, has_side_effects=True, vmem_limit_bytes=52 * 2**20
            ),
        )(tiles[0], jnp.transpose(taps, (0, 2, 3, 1)), dbias, gain, shift, expand, ebias, project, pbias, scale)
        return result[None]

    return jax.shard_map(
        body,
        mesh=mesh,
        in_specs=(
            P("section", None, "ha", "wa"),
            P(),
            P(),
            P(),
            P(),
            P(None, None, "section"),
            P(),
            P(None, "section", None),
            P(),
            P(),
        ),
        out_specs=P("section", None, "ha", "wa"),
        check_vma=False,
    )
```

```python
import functools

import jax
import jax.numpy as jnp
from jax import lax
from jax.experimental import pallas as pl
from jax.experimental.pallas import tpu as pltpu
from jax.sharding import PartitionSpec as P

EPSILON = 1e-06
MESH = pl.DeviceIdType.MESH
BF16, F32 = jnp.bfloat16, jnp.float32

AROUND = ((-1, -1), (-1, 0), (-1, 1), (0, -1), (0, 1), (1, -1), (1, 0), (1, 1))
UP, LEFT, RIGHT, DOWN = 1, 3, 4, 6
REACH = 3
ROWS = 4
DEPTH_BIAS, GAIN, SHIFT, SCALE, OFFSET = range(49, 54)
PIECE = 128


def columns_of(row):
    return jnp.broadcast_to(row, (128, row.shape[1])).T


def gelu(hidden):
    return (0.5 * hidden * (1.0 + lax.erf(hidden * (2.0**-0.5)))).astype(BF16)


def kernel(
    axis_sizes,
    tile_hbm,
    taps_hbm,
    dbias_hbm,
    gain_hbm,
    shift_hbm,
    expand_hbm,
    ebias_hbm,
    project_hbm,
    pbias_hbm,
    scale_hbm,
    out_ref,
    tile_ref,
    taps_ref,
    dbias_ref,
    gain_ref,
    shift_ref,
    expand_ref,
    ebias_ref,
    project_ref,
    pbias_ref,
    scale_ref,
    state,
    packed,
    row_halo,
    col_halo,
    ends,
    shifted,
    values,
    compact,
    wide,
    first,
    halves,
    second,
    conv,
    normed,
    active,
    projected,
    load_sem,
    send_sem,
    recv_sem,
    wsend_sem,
    wrecv_sem,
):
    blocks, rows, channels = packed.shape[0], state.shape[1], state.shape[2]
    half = halves.shape[3]
    groups, pieces = channels // 8, 2 * half // PIECE
    section, ha, wa = (lax.axis_index(a) for a in ("section", "ha", "wa"))
    n_ha, n_wa = axis_sizes
    here = []
    for dy, dx in AROUND:
        inside = jnp.bool_(True)
        if dy:
            inside = jnp.logical_and(inside, ha > 0 if dy < 0 else ha < n_ha - 1)
        if dx:
            inside = jnp.logical_and(inside, wa > 0 if dx < 0 else wa < n_wa - 1)
        here.append(inside)
    low_first = ha < n_ha // 2

    def device(d):
        dy, dx = AROUND[d]
        return (section, ha + dy, wa + dx)

    for d in range(8):

        @pl.when(jnp.logical_not(here[d]))
        def _(d=d):
            def clear(b, carry):
                if d in (UP, DOWN):
                    row_halo[b, int(d == DOWN)] = jnp.zeros(row_halo.shape[2:], BF16)
                else:
                    col_halo[b, d] = jnp.zeros(col_halo.shape[2:], BF16)
                if d in (LEFT, RIGHT):
                    col_halo[b, 5 + d] = jnp.zeros(col_halo.shape[2:], BF16)
                return carry

            lax.fori_loop(0, blocks, clear, 0)

    barrier = pltpu.get_barrier_semaphore()
    for d in range(8):

        @pl.when(here[d])
        def _(d=d):
            pl.semaphore_signal(barrier, inc=1, device_id=device(d), device_id_type=MESH)

    partner = (1 - section, ha, wa)
    pl.semaphore_signal(barrier, inc=1, device_id=partner, device_id_type=MESH)

    loads = [
        pltpu.make_async_copy(source, target, load_sem.at[k])
        for k, (source, target) in enumerate(
            (
                (tile_hbm, tile_ref),
                (expand_hbm, expand_ref),
                (ebias_hbm, ebias_ref),
                (project_hbm, project_ref),
                (taps_hbm, taps_ref),
                (dbias_hbm, dbias_ref),
                (gain_hbm, gain_ref),
                (shift_hbm, shift_ref),
                (pbias_hbm, pbias_ref),
                (scale_hbm, scale_ref),
            )
        )
    ]
    for load in loads:
        load.start()

    lane = lax.broadcasted_iota(jnp.int32, (channels, 128), 1)
    lane_group = lane // 8
    from_left = lane % 8 < REACH

    def pack(b, part):
        kept = jnp.zeros((channels, 128), BF16)
        for h in range(rows):
            kept = jnp.where(lane_group == h, pltpu.roll(state[b, h], (8 * h + REACH) % 128, 1), kept)
        packed[b, part] = kept

    def copy(b, d, part):
        place, landing = d, 7 - d
        if d == UP:
            source, target = state.at[b, pl.ds(0, REACH)], row_halo.at[b, 1]
        elif d == DOWN:
            source, target = state.at[b, pl.ds(rows - REACH, REACH)], row_halo.at[b, 0]
        else:
            if d in (LEFT, RIGHT):
                place, landing = d + 5 * part, 7 - d + 5 * part
            source, target = packed.at[b, part], col_halo.at[b, landing]
        return pltpu.make_async_remote_copy(
            src_ref=source,
            dst_ref=target,
            send_sem=send_sem.at[b, place],
            recv_sem=recv_sem.at[b, landing],
            device_id=device(d),
            device_id_type=MESH,
        )

    def start(c):
        c.start()

    def wait_send(c):
        c.wait_send()

    def each(b, which, act, part=0, condition=None):
        for d in which:

            @pl.when(here[d] if condition is None else jnp.logical_and(here[d], condition))
            def _(d=d):
                act(copy(b, d, part))

    def receive(b, which, part=0, condition=None):
        for d in which:

            @pl.when(here[d] if condition is None else jnp.logical_and(here[d], condition))
            def _(d=d):
                copy(b, 7 - d, part).wait_recv()

    loads[0].wait()
    state[0] = jnp.swapaxes(tile_ref[...], 0, 1)
    pack(0, 0)
    for load in loads[1:4]:
        load.wait()

    def prepare(b, carry):
        one = pl.ds(b, 1)
        bias = jnp.where(section == 0, ebias_ref[one, :half], ebias_ref[one, half:])
        parts = []
        for _ in range(3):
            part = bias.astype(BF16).astype(F32)
            bias = bias - part
            parts.append(part)
        whole = jnp.concatenate(
            [expand_ref[b].astype(F32)] + parts + [jnp.zeros((128 - channels - 3, half), F32)], axis=0
        )
        first[b, :half, :] = whole.T.astype(BF16)
        halves[0, b] = project_ref[b].astype(F32).T.astype(BF16)
        return carry

    lax.fori_loop(0, blocks, prepare, 0)

    greeted = jnp.int32(1)
    for d in range(8):
        greeted = greeted + here[d].astype(jnp.int32)
    pl.semaphore_wait(barrier, greeted)

    each(0, (LEFT, RIGHT, UP, DOWN, 0, 2, 5, 7), start)
    weights = [
        pltpu.make_async_remote_copy(
            src_ref=source,
            dst_ref=target,
            send_sem=wsend_sem.at[k],
            recv_sem=wrecv_sem.at[k],
            device_id=partner,
            device_id_type=MESH,
        )
        for k, (source, target) in enumerate(
            ((first.at[:, pl.ds(0, half)], first.at[:, pl.ds(half, half)]), (halves.at[0], halves.at[1]))
        )
    ]
    for c in weights:
        c.start()

    ones = lax.broadcasted_iota(jnp.int32, (128 - channels, ROWS * 128), 0) < 3
    normed[channels:, :] = jnp.where(ones, 1.0, 0.0).astype(BF16)
    normed[:channels, :] = jnp.zeros((channels, ROWS * 128), BF16)
    active[...] = jnp.zeros_like(active)
    projected[...] = jnp.zeros_like(projected)
    for load in loads[4:]:
        load.wait()

    values[...] = jnp.zeros_like(values)

    def gather(b, carry):
        one = pl.ds(b, 1)
        scale = scale_ref[one, :]
        places = [(7 * i, 7, taps_ref[b, i]) for i in range(7)]
        for k, row in enumerate(
            (dbias_ref[one, :], gain_ref[one, :], shift_ref[one, :], scale, scale * pbias_ref[one, :])
        ):
            places.append((49 + k, 1, row))
        for place, size, row in places:
            main = row.astype(BF16).astype(F32)
            values[pl.ds(place, size), :] = main
            values[pl.ds(64 + place, size), :] = row - main
        compact[b] = values[...].T.astype(BF16)
        return carry

    lax.fori_loop(0, blocks, gather, 0)
    n_values = wide.shape[0]
    every = jnp.full((128, 128), 1.0, BF16)

    def spread(b, n, count):
        kept = [jnp.where(lane % 64 == n + k, compact[b], jnp.zeros((channels, 128), BF16)) for k in range(count)]
        over = jnp.dot(jnp.concatenate(kept, axis=0), every, preferred_element_type=F32)
        wide[pl.ds(n, count)] = over.reshape(count, channels, 128)

    def lay_out(at, row):
        beyond = ends[at]
        for j in range(7):
            s = REACH - j
            if s > 0:
                moved = pltpu.roll(jnp.where(lane >= 128 - s, beyond, row), s, 1)
            elif s < 0:
                moved = pltpu.roll(jnp.where(lane < -s, beyond, row), 128 + s, 1)
            else:
                moved = row
            shifted[j, at] = moved.astype(F32)

    def lay_out_own(b, begin, chunks):
        def some(c, carry):
            for k in range(ROWS):
                h = begin + c * ROWS + k
                lay_out(REACH + h, state[b, h])
            return carry

        lax.fori_loop(0, chunks, some, 0)

    def lay_out_halo(b, side):
        both = jnp.where(from_left, col_halo[b, 5 * side], col_halo[b, 5 * side + 2])
        for k in range(REACH):
            at = side * (rows + REACH) + k
            h = jnp.where(side == 1, k, rows - REACH + k)
            ends[at] = pltpu.roll(both, 128 - REACH - 8 * h, 1)
            lay_out(at, row_halo[b, side, k])

    def conv_group(at, g):
        part = pl.ds(pl.multiple_of(g * 8, 8), 8)
        total = jnp.broadcast_to(wide[DEPTH_BIAS, part, :][None], (ROWS, 8, 128))
        for j in range(7):
            source = shifted[j, pl.ds(at, ROWS + 6), part, :]
            for i in range(7):
                total = total + source[i : i + ROWS] * wide[i * 7 + j, part, :][None]
        conv[:, part, :] = total

    def normalise():
        for k in range(ROWS):
            value = conv[k]
            centred = value - jnp.mean(value, axis=0, keepdims=True)
            variance = jnp.mean(centred * centred, axis=0, keepdims=True)
            normed[:channels, k * 128 : (k + 1) * 128] = (
                centred * lax.rsqrt(variance + EPSILON) * wide[GAIN] + wide[SHIFT]
            ).astype(BF16)

    def finish(b, at, update):
        for k in range(ROWS):
            state[b + 1, at + k] = (
                state[b, at + k].astype(F32) + wide[SCALE] * update[:, k * 128 : (k + 1) * 128] + wide[OFFSET]
            ).astype(BF16)

    def pointwise(b, at):
        hidden = jnp.dot(first[b], normed[...], preferred_element_type=F32)
        finish(b, at, jnp.dot(second[b], gelu(hidden), preferred_element_type=F32))

    def convolve_beside(b, at, before, meant):
        def piece_of(p):
            return pl.ds(pl.multiple_of(p * PIECE, PIECE), PIECE)

        def some(p, carry):
            last = piece_of(jnp.maximum(p - 1, 0))
            update = jnp.dot(second[b, :, last], active[last, :], preferred_element_type=F32)
            projected[...] = jnp.where(p > 0, projected[...] + update, 0.0)
            hidden = jnp.dot(first[b, piece_of(p), :], normed[...], preferred_element_type=F32)
            for k in range(groups // pieces):
                conv_group(at, p * (groups // pieces) + k)
            active[piece_of(p), :] = gelu(hidden)
            return carry

        lax.fori_loop(0, pieces, some, 0)

        @pl.when(meant)
        def _():
            last = piece_of(pieces - 1)
            update = jnp.dot(second[b, :, last], active[last, :], preferred_element_type=F32)
            finish(b, before, projected[...] + update)

        normalise()

    near = jnp.where(low_first, rows - ROWS, 0)
    far = rows - ROWS - near
    inner = jnp.where(low_first, rows - 2 * ROWS, ROWS)
    other = rows - ROWS - inner

    def hand_on(b, which):
        is_low = low_first == (which == 0)
        pack(b, which)
        each(b, (LEFT, RIGHT), start, which)
        each(b, (DOWN, 5, 7), start, which, is_low)
        each(b, (UP, 0, 2), start, which, jnp.logical_not(is_low))

    def block(b, carry):
        def spread_some(n, c):
            spread(b, n * 6, 6)
            return c

        lax.fori_loop(0, n_values // 6, spread_some, 0)

        @pl.when(b == 0)
        def _():
            for c in weights:
                c.wait_recv()

            def join(n, c):
                second[n] = jnp.concatenate([halves[0, n], halves[1, n]], axis=1)
                return c

            lax.fori_loop(0, blocks, join, 0)

        def chunk(k, carry):
            at = jnp.where(k == 0, inner, jnp.where(k == 1, other, jnp.where(k == 2, near, far)))
            before = jnp.where(k == 1, inner, other)
            which = k - 2

            @pl.when(jnp.logical_or(k == 0, jnp.logical_and(k == 1, b > 0)))
            def _():
                receive(b, (LEFT, RIGHT), k)
                both = jnp.where(from_left, col_halo[b, LEFT + 5 * k], col_halo[b, RIGHT + 5 * k])
                for h in range(rows):
                    ends[REACH + h] = pltpu.roll(both, 128 - (8 * h + REACH), 1)
                begin = jnp.where(k == 1, far, jnp.where(jnp.logical_and(low_first, b > 0), ROWS, 0))
                lay_out_own(b, begin, jnp.where(k == 1, 1, jnp.where(b > 0, rows // ROWS - 1, rows // ROWS)))

            @pl.when(k >= 2)
            def _():
                is_low = low_first == (which == 0)
                receive(b, (5, 6, 7), condition=is_low)
                receive(b, (0, 1, 2), condition=jnp.logical_not(is_low))
                lay_out_halo(b, jnp.where(is_low, 1, 0))

            convolve_beside(b, at, before, jnp.logical_or(k == 1, k == 2))

            @pl.when(k >= 2)
            def _():
                pointwise(b, at)

                @pl.when(b + 1 < blocks)
                def _():
                    hand_on(b + 1, which)

            return carry

        lax.fori_loop(0, 4, chunk, 0)
        return carry

    lax.fori_loop(0, blocks, block, 0)
    out_ref[...] = jnp.swapaxes(state[blocks], 0, 1)

    for c in weights:
        c.wait_send()

    def drain(b, carry):
        each(b, range(8), wait_send)
        each(b, (LEFT, RIGHT), wait_send, 1, b > 0)
        return carry

    lax.fori_loop(0, blocks, drain, 0)


def solution(mesh):
    n_ha, n_wa = mesh.shape["ha"], mesh.shape["wa"]

    def body(*arrays):
        tiles, taps, dbias, gain, shift, expand, ebias, project, pbias, scale = arrays
        blocks, channels = dbias.shape
        rows, width = tiles.shape[2:]
        half = expand.shape[2]
        operands = (tiles[0], jnp.transpose(taps, (0, 2, 3, 1)), dbias, gain, shift, expand, ebias, project, pbias, scale)
        result = pl.pallas_call(
            functools.partial(kernel, (n_ha, n_wa)),
            out_shape=jax.ShapeDtypeStruct((channels, rows, width), BF16),
            in_specs=[pl.BlockSpec(memory_space=pl.ANY)] * len(operands),
            out_specs=pl.BlockSpec(memory_space=pltpu.VMEM),
            scratch_shapes=[pltpu.VMEM(o.shape, o.dtype) for o in operands]
            + [
                pltpu.VMEM((blocks + 1, rows, channels, width), BF16),
                pltpu.VMEM((blocks, 2, channels, width), BF16),
                pltpu.VMEM((blocks, 2, REACH, channels, width), BF16),
                pltpu.VMEM((blocks, 10, channels, width), BF16),
                pltpu.VMEM((rows + 2 * REACH, channels, width), BF16),
                pltpu.VMEM((7, rows + 2 * REACH, channels, width), F32),
                pltpu.VMEM((128, channels), F32),
                pltpu.VMEM((blocks, channels, 128), BF16),
                pltpu.VMEM((54, channels, 128), F32),
                pltpu.VMEM((blocks, 2 * half, 128), BF16),
                pltpu.VMEM((2, blocks, channels, half), BF16),
                pltpu.VMEM((blocks, channels, 2 * half), BF16),
                pltpu.VMEM((ROWS, channels, width), F32),
                pltpu.VMEM((128, ROWS * width), BF16),
                pltpu.VMEM((2 * half, ROWS * width), BF16),
                pltpu.VMEM((channels, ROWS * width), F32),
                pltpu.SemaphoreType.DMA((len(operands),)),
                pltpu.SemaphoreType.DMA((blocks, 10)),
                pltpu.SemaphoreType.DMA((blocks, 10)),
                pltpu.SemaphoreType.DMA((2,)),
                pltpu.SemaphoreType.DMA((2,)),
            ],
            compiler_params=pltpu.CompilerParams(
                collective_id=0, has_side_effects=True, vmem_limit_bytes=60 * 2**20
            ),
        )(*operands)
        return result[None]

    return jax.shard_map(
        body,
        mesh=mesh,
        in_specs=(
            P("section", None, "ha", "wa"),
            P(),
            P(),
            P(),
            P(),
            P(None, None, "section"),
            P(),
            P(None, "section", None),
            P(),
            P(),
        ),
        out_specs=P("section", None, "ha", "wa"),
        check_vma=False,
    )
```

```python
import functools

import jax
import jax.numpy as jnp
from jax import lax
from jax.experimental import pallas as pl
from jax.experimental.pallas import tpu as pltpu
from jax.sharding import PartitionSpec as P

EPSILON = 1e-06
MESH = pl.DeviceIdType.MESH
BF16, F32 = jnp.bfloat16, jnp.float32

AROUND = ((-1, -1), (-1, 0), (-1, 1), (0, -1), (0, 1), (1, -1), (1, 0), (1, 1))
UP, LEFT, RIGHT, DOWN = 1, 3, 4, 6
REACH = 3
ROWS = 4
DEPTH_BIAS, GAIN, SHIFT, SCALE, OFFSET = range(49, 54)
PIECE = 128


def columns_of(row):
    return jnp.broadcast_to(row, (128, row.shape[1])).T


def gelu(hidden):
    return (0.5 * hidden * (1.0 + lax.erf(hidden * (2.0**-0.5)))).astype(BF16)


def kernel(
    axis_sizes,
    tile_hbm,
    taps_hbm,
    dbias_hbm,
    gain_hbm,
    shift_hbm,
    expand_hbm,
    ebias_hbm,
    project_hbm,
    pbias_hbm,
    scale_hbm,
    out_ref,
    tile_ref,
    taps_ref,
    dbias_ref,
    gain_ref,
    shift_ref,
    expand_ref,
    ebias_ref,
    project_ref,
    pbias_ref,
    scale_ref,
    state,
    packed,
    row_halo,
    col_halo,
    ends,
    shifted,
    values,
    compact,
    wide,
    first,
    halves,
    second,
    conv,
    normed,
    active,
    projected,
    load_sem,
    send_sem,
    recv_sem,
    wsend_sem,
    wrecv_sem,
):
    blocks, rows, channels = packed.shape[0], state.shape[1], state.shape[2]
    half = halves.shape[3]
    groups, pieces = channels // 8, 2 * half // PIECE
    section, ha, wa = (lax.axis_index(a) for a in ("section", "ha", "wa"))
    n_ha, n_wa = axis_sizes
    here = []
    for dy, dx in AROUND:
        inside = jnp.bool_(True)
        if dy:
            inside = jnp.logical_and(inside, ha > 0 if dy < 0 else ha < n_ha - 1)
        if dx:
            inside = jnp.logical_and(inside, wa > 0 if dx < 0 else wa < n_wa - 1)
        here.append(inside)
    low_first = ha < n_ha // 2

    def device(d):
        dy, dx = AROUND[d]
        return (section, ha + dy, wa + dx)

    for d in range(8):

        @pl.when(jnp.logical_not(here[d]))
        def _(d=d):
            def clear(b, carry):
                if d in (UP, DOWN):
                    row_halo[b, int(d == DOWN)] = jnp.zeros(row_halo.shape[2:], BF16)
                else:
                    col_halo[b, d] = jnp.zeros(col_halo.shape[2:], BF16)
                if d in (LEFT, RIGHT):
                    col_halo[b, 5 + d] = jnp.zeros(col_halo.shape[2:], BF16)
                return carry

            lax.fori_loop(0, blocks, clear, 0)

    barrier = pltpu.get_barrier_semaphore()
    for d in range(8):

        @pl.when(here[d])
        def _(d=d):
            pl.semaphore_signal(barrier, inc=1, device_id=device(d), device_id_type=MESH)

    partner = (1 - section, ha, wa)
    pl.semaphore_signal(barrier, inc=1, device_id=partner, device_id_type=MESH)

    loads = [
        pltpu.make_async_copy(source, target, load_sem.at[k])
        for k, (source, target) in enumerate(
            (
                (tile_hbm, tile_ref),
                (expand_hbm, expand_ref),
                (ebias_hbm, ebias_ref),
                (project_hbm, project_ref),
                (taps_hbm, taps_ref),
                (dbias_hbm, dbias_ref),
                (gain_hbm, gain_ref),
                (shift_hbm, shift_ref),
                (pbias_hbm, pbias_ref),
                (scale_hbm, scale_ref),
            )
        )
    ]
    for load in loads:
        load.start()

    lane = lax.broadcasted_iota(jnp.int32, (channels, 128), 1)
    lane_group = lane // 8
    from_left = lane % 8 < REACH

    def pack(b, part):
        kept = jnp.zeros((channels, 128), BF16)
        for h in range(rows):
            kept = jnp.where(lane_group == h, pltpu.roll(state[b, h], (8 * h + REACH) % 128, 1), kept)
        packed[b, part] = kept

    def copy(b, d, part):
        place, landing = d, 7 - d
        if d == UP:
            source, target = state.at[b, pl.ds(0, REACH)], row_halo.at[b, 1]
        elif d == DOWN:
            source, target = state.at[b, pl.ds(rows - REACH, REACH)], row_halo.at[b, 0]
        else:
            if d in (LEFT, RIGHT):
                place, landing = d + 5 * part, 7 - d + 5 * part
            source, target = packed.at[b, part], col_halo.at[b, landing]
        return pltpu.make_async_remote_copy(
            src_ref=source,
            dst_ref=target,
            send_sem=send_sem.at[b, place],
            recv_sem=recv_sem.at[b, landing],
            device_id=device(d),
            device_id_type=MESH,
        )

    def start(c):
        c.start()

    def wait_send(c):
        c.wait_send()

    def each(b, which, act, part=0, condition=None):
        for d in which:

            @pl.when(here[d] if condition is None else jnp.logical_and(here[d], condition))
            def _(d=d):
                act(copy(b, d, part))

    def receive(b, which, part=0, condition=None):
        for d in which:

            @pl.when(here[d] if condition is None else jnp.logical_and(here[d], condition))
            def _(d=d):
                copy(b, 7 - d, part).wait_recv()

    loads[0].wait()
    state[0] = jnp.swapaxes(tile_ref[...], 0, 1)
    pack(0, 0)
    greeted = jnp.int32(1)
    for d in range(8):
        greeted = greeted + here[d].astype(jnp.int32)
    pl.semaphore_wait(barrier, greeted)

    each(0, (LEFT, RIGHT, 0, 2, 5, 7, UP, DOWN), start)
    for load in loads[1:4]:
        load.wait()

    def prepare(b, carry):
        one = pl.ds(b, 1)
        bias = jnp.where(section == 0, ebias_ref[one, :half], ebias_ref[one, half:])
        parts = []
        for _ in range(3):
            part = bias.astype(BF16).astype(F32)
            bias = bias - part
            parts.append(part)
        whole = jnp.concatenate(
            [expand_ref[b].astype(F32)] + parts + [jnp.zeros((128 - channels - 3, half), F32)], axis=0
        )
        first[b, :half, :] = whole.T.astype(BF16)
        halves[0, b] = project_ref[b].astype(F32).T.astype(BF16)
        return carry

    lax.fori_loop(0, blocks, prepare, 0)

    weights = [
        pltpu.make_async_remote_copy(
            src_ref=source,
            dst_ref=target,
            send_sem=wsend_sem.at[k],
            recv_sem=wrecv_sem.at[k],
            device_id=partner,
            device_id_type=MESH,
        )
        for k, (source, target) in enumerate(
            ((first.at[:, pl.ds(0, half)], first.at[:, pl.ds(half, half)]), (halves.at[0], halves.at[1]))
        )
    ]
    for c in weights:
        c.start()

    ones = lax.broadcasted_iota(jnp.int32, (128 - channels, ROWS * 128), 0) < 3
    normed[channels:, :] = jnp.where(ones, 1.0, 0.0).astype(BF16)
    normed[:channels, :] = jnp.zeros((channels, ROWS * 128), BF16)
    active[...] = jnp.zeros_like(active)
    projected[...] = jnp.zeros_like(projected)
    for load in loads[4:]:
        load.wait()

    values[...] = jnp.zeros_like(values)

    def gather(b, carry):
        one = pl.ds(b, 1)
        scale = scale_ref[one, :]
        places = [(7 * i, 7, taps_ref[b, i]) for i in range(7)]
        for k, row in enumerate(
            (dbias_ref[one, :], gain_ref[one, :], shift_ref[one, :], scale, scale * pbias_ref[one, :])
        ):
            places.append((49 + k, 1, row))
        for place, size, row in places:
            main = row.astype(BF16).astype(F32)
            values[pl.ds(place, size), :] = main
            values[pl.ds(64 + place, size), :] = row - main
        compact[b] = values[...].T.astype(BF16)
        return carry

    lax.fori_loop(0, blocks, gather, 0)
    n_values = wide.shape[0]
    every = jnp.full((128, 128), 1.0, BF16)

    def spread(b, n, count):
        kept = [jnp.where(lane % 64 == n + k, compact[b], jnp.zeros((channels, 128), BF16)) for k in range(count)]
        over = jnp.dot(jnp.concatenate(kept, axis=0), every, preferred_element_type=F32)
        wide[pl.ds(n, count)] = over.reshape(count, channels, 128)

    def lay_out(at, row):
        beyond = ends[at]
        for j in range(7):
            s = REACH - j
            if s > 0:
                moved = pltpu.roll(jnp.where(lane >= 128 - s, beyond, row), s, 1)
            elif s < 0:
                moved = pltpu.roll(jnp.where(lane < -s, beyond, row), 128 + s, 1)
            else:
                moved = row
            shifted[j, at] = moved.astype(F32)

    def lay_out_own(b, begin, chunks):
        def some(c, carry):
            for k in range(ROWS):
                h = begin + c * ROWS + k
                lay_out(REACH + h, state[b, h])
            return carry

        lax.fori_loop(0, chunks, some, 0)

    def lay_out_halo(b, side):
        both = jnp.where(from_left, col_halo[b, 5 * side], col_halo[b, 5 * side + 2])
        for k in range(REACH):
            at = side * (rows + REACH) + k
            h = jnp.where(side == 1, k, rows - REACH + k)
            ends[at] = pltpu.roll(both, 128 - REACH - 8 * h, 1)
            lay_out(at, row_halo[b, side, k])

    def conv_group(at, g):
        part = pl.ds(pl.multiple_of(g * 8, 8), 8)
        total = jnp.broadcast_to(wide[DEPTH_BIAS, part, :][None], (ROWS, 8, 128))
        for j in range(7):
            source = shifted[j, pl.ds(at, ROWS + 6), part, :]
            for i in range(7):
                total = total + source[i : i + ROWS] * wide[i * 7 + j, part, :][None]
        conv[:, part, :] = total

    def normalise():
        for k in range(ROWS):
            value = conv[k]
            value = value - value[:1]
            average = jnp.sum(value, axis=0, keepdims=True) * (1.0 / channels)
            squares = jnp.sum(value * value, axis=0, keepdims=True) * (1.0 / channels)
            centred = value - average
            variance = jnp.maximum(squares - average * average, 0.0)
            normed[:channels, k * 128 : (k + 1) * 128] = (
                centred * lax.rsqrt(variance + EPSILON) * wide[GAIN] + wide[SHIFT]
            ).astype(BF16)

    def finish(b, at, update):
        for k in range(ROWS):
            state[b + 1, at + k] = (
                state[b, at + k].astype(F32) + wide[SCALE] * update[:, k * 128 : (k + 1) * 128] + wide[OFFSET]
            ).astype(BF16)

    def pointwise(b, at):
        kept = []
        for k in range(2):
            hidden = jnp.dot(first[b, k * half : (k + 1) * half], normed[...], preferred_element_type=F32)
            kept.append(gelu(hidden))
        finish(b, at, jnp.dot(second[b], jnp.concatenate(kept, axis=0), preferred_element_type=F32))

    def convolve_beside(b, at, before, meant):
        def piece_of(p):
            return pl.ds(pl.multiple_of(p * PIECE, PIECE), PIECE)

        def some(p, carry):
            last = piece_of(jnp.maximum(p - 1, 0))
            update = jnp.dot(second[b, :, last], active[last, :], preferred_element_type=F32)
            projected[...] = jnp.where(p > 0, projected[...] + update, 0.0)
            hidden = jnp.dot(first[b, piece_of(p), :], normed[...], preferred_element_type=F32)
            for k in range(groups // pieces):
                conv_group(at, p * (groups // pieces) + k)
            active[piece_of(p), :] = gelu(hidden)
            return carry

        lax.fori_loop(0, pieces, some, 0)

        @pl.when(meant)
        def _():
            last = piece_of(pieces - 1)
            update = jnp.dot(second[b, :, last], active[last, :], preferred_element_type=F32)
            finish(b, before, projected[...] + update)

        normalise()

    near = jnp.where(low_first, rows - ROWS, 0)
    far = rows - ROWS - near
    inner = jnp.where(low_first, rows - 2 * ROWS, ROWS)
    other = rows - ROWS - inner

    def hand_on(b, which):
        is_low = low_first == (which == 0)
        pack(b, which)
        each(b, (5, 7, DOWN), start, which, is_low)
        each(b, (0, 2, UP), start, which, jnp.logical_not(is_low))
        each(b, (LEFT, RIGHT), start, which)

    def block(b, carry):
        def spread_some(n, c):
            spread(b, n * 27, 27)
            return c

        lax.fori_loop(0, n_values // 27, spread_some, 0)

        @pl.when(b == 0)
        def _():
            for c in weights:
                c.wait_recv()

            def join(n, c):
                second[n] = jnp.concatenate([halves[0, n], halves[1, n]], axis=1)
                return c

            lax.fori_loop(0, blocks, join, 0)

        def chunk(k, carry):
            at = jnp.where(k == 0, inner, jnp.where(k == 1, other, jnp.where(k == 2, near, far)))
            before = jnp.where(k == 1, inner, other)
            which = k - 2

            @pl.when(jnp.logical_or(k == 0, jnp.logical_and(k == 1, b > 0)))
            def _():
                receive(b, (LEFT, RIGHT), k)
                both = jnp.where(from_left, col_halo[b, LEFT + 5 * k], col_halo[b, RIGHT + 5 * k])
                for h in range(rows):
                    ends[REACH + h] = pltpu.roll(both, 128 - (8 * h + REACH), 1)
                begin = jnp.where(k == 1, far, jnp.where(jnp.logical_and(low_first, b > 0), ROWS, 0))
                lay_out_own(b, begin, jnp.where(k == 1, 1, jnp.where(b > 0, rows // ROWS - 1, rows // ROWS)))

            @pl.when(k >= 2)
            def _():
                is_low = low_first == (which == 0)
                receive(b, (5, 6, 7), condition=is_low)
                receive(b, (0, 1, 2), condition=jnp.logical_not(is_low))
                lay_out_halo(b, jnp.where(is_low, 1, 0))

            convolve_beside(b, at, before, jnp.logical_or(k == 1, k == 2))

            @pl.when(k >= 2)
            def _():
                pointwise(b, at)

                @pl.when(b + 1 < blocks)
                def _():
                    hand_on(b + 1, which)

            return carry

        lax.fori_loop(0, 4, chunk, 0)
        return carry

    lax.fori_loop(0, blocks, block, 0)
    out_ref[...] = jnp.swapaxes(state[blocks], 0, 1)

    for c in weights:
        c.wait_send()

    def drain(b, carry):
        each(b, range(8), wait_send)
        each(b, (LEFT, RIGHT), wait_send, 1, b > 0)
        return carry

    lax.fori_loop(0, blocks, drain, 0)


def solution(mesh):
    n_ha, n_wa = mesh.shape["ha"], mesh.shape["wa"]

    def body(*arrays):
        tiles, taps, dbias, gain, shift, expand, ebias, project, pbias, scale = arrays
        blocks, channels = dbias.shape
        rows, width = tiles.shape[2:]
        half = expand.shape[2]
        operands = (tiles[0], jnp.transpose(taps, (0, 2, 3, 1)), dbias, gain, shift, expand, ebias, project, pbias, scale)
        result = pl.pallas_call(
            functools.partial(kernel, (n_ha, n_wa)),
            out_shape=jax.ShapeDtypeStruct((channels, rows, width), BF16),
            in_specs=[pl.BlockSpec(memory_space=pl.ANY)] * len(operands),
            out_specs=pl.BlockSpec(memory_space=pltpu.VMEM),
            scratch_shapes=[pltpu.VMEM(o.shape, o.dtype) for o in operands]
            + [
                pltpu.VMEM((blocks + 1, rows, channels, width), BF16),
                pltpu.VMEM((blocks, 2, channels, width), BF16),
                pltpu.VMEM((blocks, 2, REACH, channels, width), BF16),
                pltpu.VMEM((blocks, 10, channels, width), BF16),
                pltpu.VMEM((rows + 2 * REACH, channels, width), BF16),
                pltpu.VMEM((7, rows + 2 * REACH, channels, width), F32),
                pltpu.VMEM((128, channels), F32),
                pltpu.VMEM((blocks, channels, 128), BF16),
                pltpu.VMEM((54, channels, 128), F32),
                pltpu.VMEM((blocks, 2 * half, 128), BF16),
                pltpu.VMEM((2, blocks, channels, half), BF16),
                pltpu.VMEM((blocks, channels, 2 * half), BF16),
                pltpu.VMEM((ROWS, channels, width), F32),
                pltpu.VMEM((128, ROWS * width), BF16),
                pltpu.VMEM((2 * half, ROWS * width), BF16),
                pltpu.VMEM((channels, ROWS * width), F32),
                pltpu.SemaphoreType.DMA((len(operands),)),
                pltpu.SemaphoreType.DMA((blocks, 10)),
                pltpu.SemaphoreType.DMA((blocks, 10)),
                pltpu.SemaphoreType.DMA((2,)),
                pltpu.SemaphoreType.DMA((2,)),
            ],
            compiler_params=pltpu.CompilerParams(
                collective_id=0, has_side_effects=True, vmem_limit_bytes=60 * 2**20
            ),
        )(*operands)
        return result[None]

    return jax.shard_map(
        body,
        mesh=mesh,
        in_specs=(
            P("section", None, "ha", "wa"),
            P(),
            P(),
            P(),
            P(),
            P(None, None, "section"),
            P(),
            P(None, "section", None),
            P(),
            P(),
        ),
        out_specs=P("section", None, "ha", "wa"),
        check_vma=False,
    )
```

```python
import functools

import jax
import jax.numpy as jnp
from jax import lax
from jax.experimental import pallas as pl
from jax.experimental.pallas import tpu as pltpu
from jax.sharding import PartitionSpec as P

EPSILON = 1e-06
MESH = pl.DeviceIdType.MESH
BF16, F32 = jnp.bfloat16, jnp.float32

AROUND = ((-1, -1), (-1, 0), (-1, 1), (0, -1), (0, 1), (1, -1), (1, 0), (1, 1))
UP, LEFT, RIGHT, DOWN = 1, 3, 4, 6
REACH = 3
ROWS = 4
DEPTH_BIAS, GAIN, SHIFT, SCALE, OFFSET = range(49, 54)
PIECE = 128


def columns_of(row):
    return jnp.broadcast_to(row, (128, row.shape[1])).T


def gelu(hidden):
    return (0.5 * hidden * (1.0 + lax.erf(hidden * (2.0**-0.5)))).astype(BF16)


def kernel(
    axis_sizes,
    tile_hbm,
    taps_hbm,
    dbias_hbm,
    gain_hbm,
    shift_hbm,
    expand_hbm,
    ebias_hbm,
    project_hbm,
    pbias_hbm,
    scale_hbm,
    out_ref,
    tile_ref,
    taps_ref,
    dbias_ref,
    gain_ref,
    shift_ref,
    expand_ref,
    ebias_ref,
    project_ref,
    pbias_ref,
    scale_ref,
    state,
    packed,
    row_halo,
    col_halo,
    ends,
    shifted,
    values,
    compact,
    wide,
    first,
    halves,
    second,
    conv,
    normed,
    active,
    projected,
    load_sem,
    send_sem,
    recv_sem,
    wsend_sem,
    wrecv_sem,
):
    blocks, rows, channels = packed.shape[0], state.shape[1], state.shape[2]
    half = halves.shape[3]
    groups, pieces = channels // 8, 2 * half // PIECE
    section, ha, wa = (lax.axis_index(a) for a in ("section", "ha", "wa"))
    n_ha, n_wa = axis_sizes
    here = []
    for dy, dx in AROUND:
        inside = jnp.bool_(True)
        if dy:
            inside = jnp.logical_and(inside, ha > 0 if dy < 0 else ha < n_ha - 1)
        if dx:
            inside = jnp.logical_and(inside, wa > 0 if dx < 0 else wa < n_wa - 1)
        here.append(inside)
    low_first = ha < n_ha // 2

    def device(d):
        dy, dx = AROUND[d]
        return (section, ha + dy, wa + dx)

    for d in range(8):

        @pl.when(jnp.logical_not(here[d]))
        def _(d=d):
            def clear(b, carry):
                if d in (UP, DOWN):
                    row_halo[b, int(d == DOWN)] = jnp.zeros(row_halo.shape[2:], BF16)
                else:
                    col_halo[b, d] = jnp.zeros(col_halo.shape[2:], BF16)
                if d in (LEFT, RIGHT):
                    col_halo[b, 5 + d] = jnp.zeros(col_halo.shape[2:], BF16)
                return carry

            lax.fori_loop(0, blocks, clear, 0)

    barrier = pltpu.get_barrier_semaphore()
    for d in range(8):

        @pl.when(here[d])
        def _(d=d):
            pl.semaphore_signal(barrier, inc=1, device_id=device(d), device_id_type=MESH)

    partner = (1 - section, ha, wa)
    pl.semaphore_signal(barrier, inc=1, device_id=partner, device_id_type=MESH)

    loads = [
        pltpu.make_async_copy(source, target, load_sem.at[k])
        for k, (source, target) in enumerate(
            (
                (tile_hbm, tile_ref),
                (expand_hbm, expand_ref),
                (ebias_hbm, ebias_ref),
                (project_hbm, project_ref),
                (taps_hbm, taps_ref),
                (dbias_hbm, dbias_ref),
                (gain_hbm, gain_ref),
                (shift_hbm, shift_ref),
                (pbias_hbm, pbias_ref),
                (scale_hbm, scale_ref),
            )
        )
    ]
    for load in loads:
        load.start()

    lane = lax.broadcasted_iota(jnp.int32, (channels, 128), 1)
    lane_group = lane // 8
    from_left = lane % 8 < REACH

    def pack(b, part):
        kept = jnp.zeros((channels, 128), BF16)
        for h in range(rows):
            kept = jnp.where(lane_group == h, pltpu.roll(state[b, h], (8 * h + REACH) % 128, 1), kept)
        packed[b, part] = kept

    def copy(b, d, part):
        place, landing = d, 7 - d
        if d == UP:
            source, target = state.at[b, pl.ds(0, REACH)], row_halo.at[b, 1]
        elif d == DOWN:
            source, target = state.at[b, pl.ds(rows - REACH, REACH)], row_halo.at[b, 0]
        else:
            if d in (LEFT, RIGHT):
                place, landing = d + 5 * part, 7 - d + 5 * part
            source, target = packed.at[b, part], col_halo.at[b, landing]
        return pltpu.make_async_remote_copy(
            src_ref=source,
            dst_ref=target,
            send_sem=send_sem.at[b, place],
            recv_sem=recv_sem.at[b, landing],
            device_id=device(d),
            device_id_type=MESH,
        )

    def start(c):
        c.start()

    def wait_send(c):
        c.wait_send()

    def each(b, which, act, part=0, condition=None):
        for d in which:

            @pl.when(here[d] if condition is None else jnp.logical_and(here[d], condition))
            def _(d=d):
                act(copy(b, d, part))

    def receive(b, which, part=0, condition=None):
        for d in which:

            @pl.when(here[d] if condition is None else jnp.logical_and(here[d], condition))
            def _(d=d):
                copy(b, 7 - d, part).wait_recv()

    loads[0].wait()
    state[0] = jnp.swapaxes(tile_ref[...], 0, 1)
    pack(0, 0)
    greeted = jnp.int32(1)
    for d in range(8):
        greeted = greeted + here[d].astype(jnp.int32)
    pl.semaphore_wait(barrier, greeted)

    each(0, (LEFT, RIGHT, 0, 2, 5, 7, UP, DOWN), start)
    for load in loads[1:4]:
        load.wait()

    def prepare(b, carry):
        one = pl.ds(b, 1)
        bias = jnp.where(section == 0, ebias_ref[one, :half], ebias_ref[one, half:])
        parts = []
        for _ in range(3):
            part = bias.astype(BF16).astype(F32)
            bias = bias - part
            parts.append(part)
        whole = jnp.concatenate(
            [expand_ref[b].astype(F32)] + parts + [jnp.zeros((128 - channels - 3, half), F32)], axis=0
        )
        first[b, :half, :] = whole.T.astype(BF16)
        halves[0, b] = project_ref[b].astype(F32).T.astype(BF16)
        return carry

    lax.fori_loop(0, blocks, prepare, 0)

    weights = [
        pltpu.make_async_remote_copy(
            src_ref=source,
            dst_ref=target,
            send_sem=wsend_sem.at[k],
            recv_sem=wrecv_sem.at[k],
            device_id=partner,
            device_id_type=MESH,
        )
        for k, (source, target) in enumerate(
            ((first.at[:, pl.ds(0, half)], first.at[:, pl.ds(half, half)]), (halves.at[0], halves.at[1]))
        )
    ]
    for c in weights:
        c.start()

    ones = lax.broadcasted_iota(jnp.int32, (128 - channels, ROWS * 128), 0) < 3
    normed[channels:, :] = jnp.where(ones, 1.0, 0.0).astype(BF16)
    normed[:channels, :] = jnp.zeros((channels, ROWS * 128), BF16)
    active[...] = jnp.zeros_like(active)
    projected[...] = jnp.zeros_like(projected)
    for load in loads[4:]:
        load.wait()

    values[...] = jnp.zeros_like(values)

    def gather(b, carry):
        one = pl.ds(b, 1)
        scale = scale_ref[one, :]
        places = [(7 * i, 7, taps_ref[b, i]) for i in range(7)]
        for k, row in enumerate(
            (dbias_ref[one, :], gain_ref[one, :], shift_ref[one, :], scale, scale * pbias_ref[one, :])
        ):
            places.append((49 + k, 1, row))
        for place, size, row in places:
            main = row.astype(BF16).astype(F32)
            values[pl.ds(place, size), :] = main
            values[pl.ds(64 + place, size), :] = row - main
        compact[b] = values[...].T.astype(BF16)
        return carry

    lax.fori_loop(0, blocks, gather, 0)
    n_values = wide.shape[0]
    every = jnp.full((128, 128), 1.0, BF16)

    def spread(b, n, count):
        kept = [jnp.where(lane % 64 == n + k, compact[b], jnp.zeros((channels, 128), BF16)) for k in range(count)]
        over = jnp.dot(jnp.concatenate(kept, axis=0), every, preferred_element_type=F32)
        wide[pl.ds(n, count)] = over.reshape(count, channels, 128)

    def lay_out(at, row):
        beyond = ends[at]
        for j in range(7):
            s = REACH - j
            if s > 0:
                moved = pltpu.roll(jnp.where(lane >= 128 - s, beyond, row), s, 1)
            elif s < 0:
                moved = pltpu.roll(jnp.where(lane < -s, beyond, row), 128 + s, 1)
            else:
                moved = row
            shifted[j, at] = moved.astype(F32)

    def lay_out_own(b, begin, chunks):
        def some(c, carry):
            for k in range(ROWS):
                h = begin + c * ROWS + k
                lay_out(REACH + h, state[b, h])
            return carry

        lax.fori_loop(0, chunks, some, 0)

    def lay_out_halo(b, side):
        both = jnp.where(from_left, col_halo[b, 5 * side], col_halo[b, 5 * side + 2])
        for k in range(REACH):
            at = side * (rows + REACH) + k
            h = jnp.where(side == 1, k, rows - REACH + k)
            ends[at] = pltpu.roll(both, 128 - REACH - 8 * h, 1)
            lay_out(at, row_halo[b, side, k])

    def conv_group(at, g):
        part = pl.ds(pl.multiple_of(g * 8, 8), 8)
        total = jnp.broadcast_to(wide[DEPTH_BIAS, part, :][None], (ROWS, 8, 128))
        for j in range(7):
            source = shifted[j, pl.ds(at, ROWS + 6), part, :]
            for i in range(7):
                total = total + source[i : i + ROWS] * wide[i * 7 + j, part, :][None]
        conv[:, part, :] = total

    def normalise():
        for k in range(ROWS):
            value = conv[k]
            value = value - value[:1]
            average = jnp.sum(value, axis=0, keepdims=True) * (1.0 / channels)
            squares = jnp.sum(value * value, axis=0, keepdims=True) * (1.0 / channels)
            centred = value - average
            variance = jnp.maximum(squares - average * average, 0.0)
            normed[:channels, k * 128 : (k + 1) * 128] = (
                centred * lax.rsqrt(variance + EPSILON) * wide[GAIN] + wide[SHIFT]
            ).astype(BF16)

    def finish(b, at, update):
        for k in range(ROWS):
            state[b + 1, at + k] = (
                state[b, at + k].astype(F32) + wide[SCALE] * update[:, k * 128 : (k + 1) * 128] + wide[OFFSET]
            ).astype(BF16)

    def pointwise(b, at):
        kept = []
        for k in range(2):
            hidden = jnp.dot(first[b, k * half : (k + 1) * half], normed[...], preferred_element_type=F32)
            kept.append(gelu(hidden))
        finish(b, at, jnp.dot(second[b], jnp.concatenate(kept, axis=0), preferred_element_type=F32))

    def convolve_beside(b, at, before, meant):
        def piece_of(p):
            return pl.ds(pl.multiple_of(p * PIECE, PIECE), PIECE)

        def some(p, carry):
            last = piece_of(jnp.maximum(p - 1, 0))
            update = jnp.dot(second[b, :, last], active[last, :], preferred_element_type=F32)
            projected[...] = jnp.where(p > 0, projected[...] + update, 0.0)
            hidden = jnp.dot(first[b, piece_of(p), :], normed[...], preferred_element_type=F32)
            early = groups // pieces // 2
            for k in range(early):
                conv_group(at, p * (groups // pieces) + k)
            active[piece_of(p), :] = gelu(hidden)
            for k in range(early, groups // pieces):
                conv_group(at, p * (groups // pieces) + k)
            return carry

        lax.fori_loop(0, pieces, some, 0)

        @pl.when(meant)
        def _():
            last = piece_of(pieces - 1)
            update = jnp.dot(second[b, :, last], active[last, :], preferred_element_type=F32)
            finish(b, before, projected[...] + update)

        normalise()

    near = jnp.where(low_first, rows - ROWS, 0)
    far = rows - ROWS - near
    inner = jnp.where(low_first, rows - 2 * ROWS, ROWS)
    other = rows - ROWS - inner

    def hand_on(b, which):
        is_low = low_first == (which == 0)
        pack(b, which)
        each(b, (5, 7, DOWN), start, which, is_low)
        each(b, (0, 2, UP), start, which, jnp.logical_not(is_low))
        each(b, (LEFT, RIGHT), start, which)

    def block(b, carry):
        def spread_some(n, c):
            spread(b, n * 27, 27)
            return c

        lax.fori_loop(0, n_values // 27, spread_some, 0)

        @pl.when(b == 0)
        def _():
            for c in weights:
                c.wait_recv()

            def join(n, c):
                second[n] = jnp.concatenate([halves[0, n], halves[1, n]], axis=1)
                return c

            lax.fori_loop(0, blocks, join, 0)

        def chunk(k, carry):
            which = jnp.where(b + 1 == blocks, 3 - k, k - 2)
            at = jnp.where(k == 0, inner, jnp.where(k == 1, other, jnp.where(which == 0, near, far)))
            before = jnp.where(k == 1, inner, other)

            @pl.when(jnp.logical_or(k == 0, jnp.logical_and(k == 1, b > 0)))
            def _():
                receive(b, (LEFT, RIGHT), k)
                both = jnp.where(from_left, col_halo[b, LEFT + 5 * k], col_halo[b, RIGHT + 5 * k])
                for h in range(rows):
                    ends[REACH + h] = pltpu.roll(both, 128 - (8 * h + REACH), 1)
                begin = jnp.where(k == 1, far, jnp.where(jnp.logical_and(low_first, b > 0), ROWS, 0))
                lay_out_own(b, begin, jnp.where(k == 1, 1, jnp.where(b > 0, rows // ROWS - 1, rows // ROWS)))

            @pl.when(k >= 2)
            def _():
                is_low = low_first == (which == 0)
                receive(b, (5, 6, 7), condition=is_low)
                receive(b, (0, 1, 2), condition=jnp.logical_not(is_low))
                lay_out_halo(b, jnp.where(is_low, 1, 0))

            convolve_beside(b, at, before, jnp.logical_or(k == 1, k == 2))

            @pl.when(k >= 2)
            def _():
                pointwise(b, at)

                @pl.when(b + 1 < blocks)
                def _():
                    hand_on(b + 1, which)

            return carry

        lax.fori_loop(0, 4, chunk, 0)
        return carry

    lax.fori_loop(0, blocks, block, 0)
    out_ref[...] = jnp.swapaxes(state[blocks], 0, 1)

    for c in weights:
        c.wait_send()

    def drain(b, carry):
        each(b, range(8), wait_send)
        each(b, (LEFT, RIGHT), wait_send, 1, b > 0)
        return carry

    lax.fori_loop(0, blocks, drain, 0)


def solution(mesh):
    n_ha, n_wa = mesh.shape["ha"], mesh.shape["wa"]

    def body(*arrays):
        tiles, taps, dbias, gain, shift, expand, ebias, project, pbias, scale = arrays
        blocks, channels = dbias.shape
        rows, width = tiles.shape[2:]
        half = expand.shape[2]
        operands = (tiles[0], jnp.transpose(taps, (0, 2, 3, 1)), dbias, gain, shift, expand, ebias, project, pbias, scale)
        result = pl.pallas_call(
            functools.partial(kernel, (n_ha, n_wa)),
            out_shape=jax.ShapeDtypeStruct((channels, rows, width), BF16),
            in_specs=[pl.BlockSpec(memory_space=pl.ANY)] * len(operands),
            out_specs=pl.BlockSpec(memory_space=pltpu.VMEM),
            scratch_shapes=[pltpu.VMEM(o.shape, o.dtype) for o in operands]
            + [
                pltpu.VMEM((blocks + 1, rows, channels, width), BF16),
                pltpu.VMEM((blocks, 2, channels, width), BF16),
                pltpu.VMEM((blocks, 2, REACH, channels, width), BF16),
                pltpu.VMEM((blocks, 10, channels, width), BF16),
                pltpu.VMEM((rows + 2 * REACH, channels, width), BF16),
                pltpu.VMEM((7, rows + 2 * REACH, channels, width), F32),
                pltpu.VMEM((128, channels), F32),
                pltpu.VMEM((blocks, channels, 128), BF16),
                pltpu.VMEM((54, channels, 128), F32),
                pltpu.VMEM((blocks, 2 * half, 128), BF16),
                pltpu.VMEM((2, blocks, channels, half), BF16),
                pltpu.VMEM((blocks, channels, 2 * half), BF16),
                pltpu.VMEM((ROWS, channels, width), F32),
                pltpu.VMEM((128, ROWS * width), BF16),
                pltpu.VMEM((2 * half, ROWS * width), BF16),
                pltpu.VMEM((channels, ROWS * width), F32),
                pltpu.SemaphoreType.DMA((len(operands),)),
                pltpu.SemaphoreType.DMA((blocks, 10)),
                pltpu.SemaphoreType.DMA((blocks, 10)),
                pltpu.SemaphoreType.DMA((2,)),
                pltpu.SemaphoreType.DMA((2,)),
            ],
            compiler_params=pltpu.CompilerParams(
                collective_id=0, has_side_effects=True, vmem_limit_bytes=60 * 2**20
            ),
        )(*operands)
        return result[None]

    return jax.shard_map(
        body,
        mesh=mesh,
        in_specs=(
            P("section", None, "ha", "wa"),
            P(),
            P(),
            P(),
            P(),
            P(None, None, "section"),
            P(),
            P(None, "section", None),
            P(),
            P(),
        ),
        out_specs=P("section", None, "ha", "wa"),
        check_vma=False,
    )
```
